32 devices in a mesh: row: 2 (over x), col: 4 (over z), layer: 4 (over y, core).
Axes of the slice: x: 2, y: 2, z: 4, core: 2. Of those that a mesh axis runs over, the one named last changes fastest.
Arguments:
- amplitudes: float32 [1024, 2048], P('row', ('col', 'layer')), may hold values from -6 to 6
- integrals: float32 [2048, 16384], P(('row', 'layer'), 'col'), may hold values from -0.125 to 0.125
Outputs:
- ladder: float32 [1024, 16384], P('row', ('col', 'layer'))
The draws below stay inside these ranges and needn't reach their ends.
All inputs are finite; a program needn't handle non-finite values.
Results may differ from the reference program's by a relative error of at most 0.000082.
Values sent between devices are 32-bit elements; how exact they have to be, the bound alone decides.
No kernel may reach another device: no remote copies, remote signals or barrier semaphores. Data moves between devices by JAX's collectives and lax.ppermute only.
A program may use at most 64 MiB of HBM per device.

```python
import jax
import jax.numpy as jnp
from jax import lax

CONTR = 2048
OUTW = 16384
ROWS = 1024


def block_scale(rng, extent, pieces, low, largest):
    level = 1.0
    for axis_at, blocks in pieces:
        steps = jax.random.uniform(jax.random.fold_in(jax.random.fold_in(rng, 6), axis_at), (blocks,), jnp.float32, low / len(pieces), largest / len(pieces))
        level = level * jnp.repeat(jnp.exp(steps), extent[axis_at] // blocks).reshape((-1,) + (1,) * (len(extent) - 1 - axis_at))
    return level


def centred(stream_key, shape, width, bound, cuts=(), dtype=jnp.bfloat16):
    gain = block_scale(stream_key, shape, cuts, -0.22, 0.18) if cuts else 1.0
    values = jax.random.normal(stream_key, shape, jnp.float32) * width * gain
    return jnp.minimum(jnp.maximum(values, -bound), bound).astype(dtype)


def setup_inputs(seed: int = 0) -> dict:
    key_list = jax.random.split(jax.random.key(seed), 3)
    amplitudes = centred(key_list[0], (ROWS, CONTR), 1.0, 6.0, ((0, 2), (1, 16)), jnp.float32)
    integrals = centred(key_list[1], (CONTR, OUTW), CONTR ** -0.5, 0.125, ((0, 8), (1, 4)), jnp.float32)
    return {"amplitudes": amplitudes, "integrals": integrals}


def reference(amplitudes, integrals):
    product = jnp.dot(amplitudes, integrals, precision=lax.Precision.HIGHEST, preferred_element_type=jnp.float32)
    return 0.5 * product
```

```python
import jax
import jax.numpy as jnp
from jax import lax
from jax.experimental import pallas as pl
from jax.experimental.pallas import tpu as pltpu
from jax.sharding import PartitionSpec as P

AXES = ("row", "col", "layer")
F32, BF16 = jnp.float32, jnp.bfloat16


def gather_plan(amplitudes, integrals):
    amp_panel = lax.all_gather(amplitudes, "layer", axis=1, tiled=True)
    amp_whole = lax.all_gather(amp_panel, "col", axis=1, tiled=True)
    int_mine = lax.all_to_all(integrals, "layer", split_axis=1, concat_axis=0, tiled=True)
    product = jnp.dot(
        amp_whole,
        lax.all_gather(int_mine, "row", axis=0, tiled=True),
        precision=lax.Precision.HIGHEST,
        preferred_element_type=F32,
    )
    return 0.5 * product


def split(value):
    high = value.astype(BF16)
    return high, (value - high.astype(F32)).astype(BF16)


def prep_kernel(place, b0, b1, b2, b3, twin, high, low):
    p, y, core = place[0], place[1], place[2]
    kb = b0.shape[1]
    for rel, mine in enumerate((b0, b1, b2, b3)):
        slot = (p ^ (rel >> 1)) * 2 + (y ^ (rel & 1))
        for value, at in ((mine[...], core), (twin[rel], 1 - core)):
            h, l = split(value)
            high[slot, :, pl.ds(pl.multiple_of(at * kb, kb), kb)] = h
            low[slot, :, pl.ds(pl.multiple_of(at * kb, kb), kb)] = l


def prep(place, blocks, twin):
    rows, kb = blocks[0].shape
    shape = jax.ShapeDtypeStruct((4, rows, 2 * kb), BF16)
    return pl.pallas_call(
        prep_kernel,
        out_shape=(shape, shape),
        in_specs=[pl.BlockSpec(memory_space=pltpu.SMEM)] + [pl.BlockSpec(memory_space=pltpu.VMEM)] * 5,
        out_specs=(pl.BlockSpec(memory_space=pltpu.VMEM),) * 2,
        cost_estimate=pl.CostEstimate(flops=0, bytes_accessed=64 * rows * kb, transcendentals=0),
        name="prep",
    )(place, *blocks, twin)


def mul_kernel(place, high, low, c0, c1, c2, c3, out):
    layer = place[3]
    total = jnp.zeros(out.shape, F32)
    for rel, piece in enumerate((c0, c1, c2, c3)):
        slot = layer ^ rel
        bh, bl = split(piece[...])
        ah, al = high[slot], low[slot]
        total += jnp.dot(ah, bh, preferred_element_type=F32)
        total += jnp.dot(ah, bl, preferred_element_type=F32)
        total += jnp.dot(al, bh, preferred_element_type=F32)
    out[...] = total


def mul(place, amp, pieces):
    high, low = amp
    rows, n = high.shape[1], pieces[0].shape[1]
    k = high.shape[0] * high.shape[2]
    return pl.pallas_call(
        mul_kernel,
        out_shape=jax.ShapeDtypeStruct((rows, n), F32),
        in_specs=[pl.BlockSpec(memory_space=pltpu.SMEM)] + [pl.BlockSpec(memory_space=pltpu.VMEM)] * 6,
        out_specs=pl.BlockSpec(memory_space=pltpu.VMEM),
        cost_estimate=pl.CostEstimate(flops=6 * rows * n * k, bytes_accessed=4 * (rows * k + n * k + rows * n), transcendentals=0),
        name="mul",
    )(place, high, low, *pieces)


def add_kernel(mine, other, *refs):
    refs[-1][...] = 0.5 * (mine[...] + other[...])


def put(whole, mine, other, at, width):
    rows, n = mine.shape
    tile = 128
    spec = pl.BlockSpec((rows, tile), lambda g: (0, g))
    last = [] if whole is None else [whole]
    return pl.pallas_call(
        add_kernel,
        grid=(n // tile,),
        out_shape=jax.ShapeDtypeStruct((rows, width), F32),
        in_specs=[spec, spec] + [pl.BlockSpec(memory_space=pl.ANY)] * len(last),
        out_specs=pl.BlockSpec((rows, tile), lambda g: (0, at // tile + g)),
        input_output_aliases={2: 0} if last else {},
        cost_estimate=pl.CostEstimate(flops=2 * rows * n, bytes_accessed=12 * rows * n, transcendentals=0),
        name="put",
    )(mine, other, *last)


def swap_plan(C, L, cuts):
    half = C // 2
    every = [(r, c, l) for r in range(2) for c in range(C) for l in range(L)]

    def flat(r, c, l):
        return (r * C + c) * L + l

    def send(value, where, who=lambda r, c, l: True):
        return lax.ppermute(value, AXES, [(flat(*d), flat(*where(*d))) for d in every if who(*d)])

    def home(r, c, l):
        return c // half == r

    def shards(amplitudes, integrals):
        r, c, l = (lax.axis_index(a) for a in AXES)
        here = c // half == r
        place = jnp.stack([c % half, l // 2, l % 2, l]).astype(jnp.int32)
        width = integrals.shape[1] // L

        def piece(rel, at, n):
            return lax.dynamic_slice_in_dim(integrals, (l ^ rel) * width + at, n, 1)

        first = send(amplitudes, lambda r, c, l: (r, (c + half) % C, l) if home(r, c, l) else (1 - r, c, l))
        second = send(amplitudes, lambda r, c, l: (1 - r, (c + half) % C, l), lambda r, c, l: not home(r, c, l))
        turned = send(amplitudes, lambda r, c, l: (r, c, l ^ 2), home)
        other = jnp.where(here, first, second)
        blocks = [other] + [
            send(other, lambda r, c, l, p=p, y=y: (r, c ^ p, l ^ (2 * y))) for p, y in ((0, 1), (1, 0), (1, 1))
        ]
        far = prep(place, blocks, send(jnp.stack(blocks), lambda r, c, l: (r, c, l ^ 1)))

        turned = jnp.where(here, turned, send(turned, lambda r, c, l: (r, (c + half) % C, l), home))
        own = jnp.stack([jnp.where(here, amplitudes, first), turned])
        pair = send(own, lambda r, c, l: (r, c ^ 1, l))
        blocks = [own[0], own[1], pair[0], pair[1]]
        near = prep(place, blocks, send(jnp.stack(blocks), lambda r, c, l: (r, c, l ^ 1)))

        whole = None
        at = 0
        for n in cuts:
            pieces = [piece(0, at, n)]
            for rel in (1, 2, 3):
                pieces.append(send(piece(rel, at, n), lambda r, c, l: (r, c, l ^ rel)))
            got = send(mul(place, far, pieces), lambda r, c, l: (1 - r, c, l))
            whole = put(whole, mul(place, near, pieces), got, at, width)
            at += n
        return whole

    return shards


def solution(mesh):
    in_specs = (P("row", ("col", "layer")), P(("row", "layer"), "col"))
    out_specs = P("row", ("col", "layer"))
    R, C, L = (mesh.shape[a] for a in AXES)
    plan = swap_plan(C, L, (256,) * 4) if (R, C, L) == (2, 4, 4) else gather_plan
    return jax.shard_map(plan, mesh=mesh, in_specs=in_specs, out_specs=out_specs, check_vma=False)
```

```python
import jax
import jax.numpy as jnp
from jax import lax
from jax.experimental import pallas as pl
from jax.experimental.pallas import tpu as pltpu
from jax.sharding import PartitionSpec as P

AXES = ("row", "col", "layer")
F32, BF16 = jnp.float32, jnp.bfloat16
SMEM = pl.BlockSpec(memory_space=pltpu.SMEM)
ANY = pl.BlockSpec(memory_space=pltpu.HBM)
FREE = pl.CostEstimate(flops=0, bytes_accessed=0, transcendentals=0)
OWN = 0
DEPTH = 3
LAG = 2
MOVED = 3
PAIR = 7
CUTLIM = 62
JOINLIM = 32


def gather_plan(amplitudes, integrals):
    amp_panel = lax.all_gather(amplitudes, "layer", axis=1, tiled=True)
    amp_whole = lax.all_gather(amp_panel, "col", axis=1, tiled=True)
    int_mine = lax.all_to_all(integrals, "layer", split_axis=1, concat_axis=0, tiled=True)
    product = jnp.dot(
        amp_whole,
        lax.all_gather(int_mine, "row", axis=0, tiled=True),
        precision=lax.Precision.HIGHEST,
        preferred_element_type=F32,
    )
    return 0.5 * product


def after(value, *done):
    return lax.optimization_barrier((value, *done))[0]


def split(value):
    high = value.astype(BF16)
    return high, (value - high.astype(F32)).astype(BF16)


def copies(pairs, sems):
    made = [pltpu.make_async_copy(src, dst, sems.at[i]) for i, (src, dst) in enumerate(pairs)]
    for copy in made:
        copy.start()
    return made


def cut(integrals, wanted, limit):
    rows, width = integrals.shape[0], integrals.shape[1] // 4
    wide = [sum(n for _, _, n in parts) for parts in wanted]

    def kernel(source, *refs):
        layer = lax.axis_index("layer")
        pairs = []
        for parts, out in zip(wanted, refs):
            to = 0
            for rel, at, n in parts:
                pairs.append((source.at[:, pl.ds(pl.multiple_of((layer ^ rel) * width + at, 128), n)], out.at[:, pl.ds(to, n)]))
                to += n
        for copy in copies(pairs, refs[-1]):
            copy.wait()

    return pl.pallas_call(
        kernel,
        out_shape=[jax.ShapeDtypeStruct((rows, n), F32) for n in wide],
        in_specs=[ANY],
        out_specs=[pl.BlockSpec(memory_space=pltpu.VMEM)] * len(wanted),
        scratch_shapes=[pltpu.SemaphoreType.DMA((sum(len(parts) for parts in wanted),))],
        compiler_params=pltpu.CompilerParams(vmem_limit_bytes=limit << 20),
        cost_estimate=FREE,
        name="cut",
    )(integrals)


def join(integrals, twin, cuts):
    rows, width = integrals.shape[0], integrals.shape[1] // 4

    def kernel(source, theirs, *refs):
        layer = lax.axis_index("layer")
        pairs = []
        for (at, n), out in zip(cuts, refs):
            pairs.append((source.at[:, pl.ds(pl.multiple_of((layer ^ 2) * width + at, 128), n)], out.at[:rows]))
            pairs.append((theirs.at[:, pl.ds(width + at - cuts[0][0], n)], out.at[rows:]))
        for copy in copies(pairs, refs[-1]):
            copy.wait()

    return pl.pallas_call(
        kernel,
        out_shape=[jax.ShapeDtypeStruct((2 * rows, n), F32) for _, n in cuts],
        in_specs=[ANY] * 2,
        out_specs=[pl.BlockSpec(memory_space=pltpu.VMEM)] * len(cuts),
        scratch_shapes=[pltpu.SemaphoreType.DMA((2 * len(cuts),))],
        compiler_params=pltpu.CompilerParams(vmem_limit_bytes=JOINLIM << 20),
        cost_estimate=FREE,
        name="join",
    )(integrals, twin)


def mul(token, blocks, twin, integrals, near, pieces, at, scale):
    _, rows, kb = blocks.shape
    depth, width = integrals.shape[0], integrals.shape[1] // 4
    k = 8 * kb
    n = sum(piece[0].shape[1] for piece in pieces)
    flat = [part for piece in pieces for part in piece]
    count = 8 + 2 * (len(pieces) + 1)

    def kernel(turn, mine, other, source, c1, *refs):
        out, turned, a, b, sems = refs[len(flat) :]
        turned[0] = turn[0]
        layer, p = lax.axis_index("layer"), lax.axis_index("col") % 2
        y, core = layer // 2, layer % 2

        def rows_of(rel):
            return pl.ds(pl.multiple_of((layer ^ rel) * depth, depth), depth)

        pairs = [(source.at[:, pl.ds(pl.multiple_of(layer * width + at, 128), n)], b.at[rows_of(0), :])]
        pairs.append((c1.at[:, pl.ds(at, n)], b.at[rows_of(1), :]))
        to, rest = 0, list(refs)
        for piece in pieces:
            got = [rest.pop(0) for _ in piece]
            wide = piece[0].shape[1]
            c2, c3 = got if len(got) == 2 else (got[0].at[:depth], got[0].at[depth:])
            pairs += [(c2, b.at[rows_of(2), pl.ds(to, wide)]), (c3, b.at[rows_of(3), pl.ds(to, wide)])]
            to += wide
        for rel in range(4):
            slot = (p ^ (rel >> 1)) * 2 + (y ^ (rel & 1))
            for ref, where in ((mine, core), (other, 1 - core)):
                lanes = pl.ds(pl.multiple_of((slot * 2 + where) * kb, kb), kb)
                pairs.append((ref.at[rel], a.at[:, lanes]))
        for copy in copies(pairs, sems):
            copy.wait()
        ah, al = split(a[...])
        for first in range(0, n, 256):
            lanes = pl.ds(first, min(256, n - first))
            bh, bl = split(b[:, lanes])
            out[:, lanes] = scale * (
                jnp.dot(ah, bh, preferred_element_type=F32)
                + jnp.dot(ah, bl, preferred_element_type=F32)
                + jnp.dot(al, bh, preferred_element_type=F32)
            )

    return pl.pallas_call(
        kernel,
        out_shape=(jax.ShapeDtypeStruct((rows, n), F32), jax.ShapeDtypeStruct((1,), jnp.int32)),
        in_specs=[SMEM] + [ANY] * (4 + len(flat)),
        out_specs=(pl.BlockSpec(memory_space=pltpu.VMEM), SMEM),
        scratch_shapes=[pltpu.VMEM((rows, k), F32), pltpu.VMEM((k, n), F32), pltpu.SemaphoreType.DMA((count,))],
        compiler_params=pltpu.CompilerParams(vmem_limit_bytes=24 << 20),
        cost_estimate=FREE,
        name="mul",
    )(token, blocks, twin, integrals, near, *flat)


def add(token, mine, others):
    rows, width = mine.shape
    starts = [sum(o.shape[1] for o in others[:i]) for i in range(len(others))]

    def kernel(turn, a, *refs):
        sources, out, total, sems = refs[: len(others)], refs[-3], refs[-2], refs[-1]
        made = []
        for i, (source, at) in enumerate(zip(sources, starts)):
            lanes = pl.ds(at, others[i].shape[1])
            total[:, lanes] = a[:, lanes] + 0.5 * source[...]
            made.append(pltpu.make_async_copy(total.at[:, lanes], out.at[:, lanes], sems.at[i]))
            made[-1].start()
        for copy in made:
            copy.wait()

    return pl.pallas_call(
        kernel,
        out_shape=jax.ShapeDtypeStruct((rows, width), F32),
        in_specs=[SMEM] + [pl.BlockSpec(memory_space=pltpu.VMEM)] * (1 + len(others)),
        out_specs=ANY,
        scratch_shapes=[pltpu.VMEM((rows, width), F32), pltpu.SemaphoreType.DMA((len(others),))],
        compiler_params=pltpu.CompilerParams(vmem_limit_bytes=24 << 20),
        cost_estimate=FREE,
        name="add",
    )(token, mine, *others)


def swap_plan(C, L, cuts):
    half = C // 2
    every = [(r, c, l) for r in range(2) for c in range(C) for l in range(L)]

    def flat(r, c, l):
        return (r * C + c) * L + l

    def send(value, where, who=lambda r, c, l: True):
        return lax.ppermute(value, AXES, [(flat(*d), flat(*where(*d))) for d in every if who(*d)])

    def home(r, c, l):
        return c // half == r

    def away(r, c, l):
        return c // half != r

    def shards(amplitudes, integrals):
        r, c, l = (lax.axis_index(a) for a in AXES)
        here = c // half == r
        width = integrals.shape[1] // L
        starts = [sum(cuts[:i]) for i in range(len(cuts))]
        last = len(cuts) - 1
        v = {"turn": r.reshape(1).astype(jnp.int32)}

        def tick(*names):
            names = ("turn", *names)
            v.update(zip(names, lax.optimization_barrier([v[name] for name in names])))

        def now(*names):
            tick(*names)
            return v[names[0]] if len(names) == 1 else [v[name] for name in names]

        def twin_of(value):
            return send(value, lambda r, c, l: (r, c, l ^ 1))

        def far_sum(i):
            part, v["turn"] = mul(v["turn"], *v["far"], integrals, v["near_twin"], [v["b", i]], starts[i], 1.0)
            v["sum", i] = send(part, lambda r, c, l: (1 - r, c, l))

        def go(i):
            v["b", i] = [send(now(("slab", i)), lambda r, c, l: (r, c, l ^ 2))]

        v["straight"] = send(amplitudes, lambda r, c, l: (1 - r, c, l), away)
        v["slant"] = send(amplitudes, lambda r, c, l: (1 - r, (c + half) % C, l), away)
        *first, rest = cut(integrals, [[(rel, 0, cuts[0])] for rel in (2, 3)] + [[(1, 0, width), (3, cuts[0], width - cuts[0])]], CUTLIM)
        v["b", 0] = [send(part, lambda r, c, l, rel=rel: (r, c, l ^ rel)) for rel, part in zip((2, 3), first)]
        v["rest"], v["amp"] = lax.optimization_barrier((rest, amplitudes))
        v["turned"] = send(v["amp"], lambda r, c, l: (r, c, l ^ 2), home)
        tick("straight", "slant", ("b", 0), "turned", "rest", "amp")
        other = jnp.where(here, v["straight"], v["slant"])
        v["blocks"] = [other] + [
            send(other, lambda r, c, l, p=p, y=y: (r, c ^ p, l ^ (2 * y))) for p, y in ((0, 1), (1, 0), (1, 1))
        ]
        v["near_twin"] = twin_of(v["rest"])
        slabs = join(integrals, v["near_twin"], [(starts[i], cuts[i]) for i in range(1, last + 1)])
        v.update({("slab", i + 1): slab for i, slab in enumerate(slabs)})
        tick("blocks", "near_twin", "turned", "amp", *[("slab", i) for i in range(1, last + 1)])
        far = jnp.stack(v["blocks"])
        v["far"] = [far, twin_of(far)]
        for i in range(1, DEPTH):
            go(i)
        tick("far")
        for i in range(last + 1):
            if i:
                tick(("b", i))
            if i + DEPTH <= last:
                go(i + DEPTH)
            far_sum(i)
            if i == OWN:
                v["own"] = jnp.stack(now("amp", "turned"))
                v["moved"] = send(v["own"], lambda r, c, l: (r, (c + half) % C, l), home)
            if i >= LAG:
                tick(("sum", i - LAG))
            if i == MOVED:
                tick("moved")
                v["own"] = jnp.where(here, *now("own", "moved"))
                v["pair"] = send(v["own"], lambda r, c, l: (r, c ^ 1, l))
            if i == PAIR:
                tick("pair")
                near = jnp.concatenate(now("own", "pair"))
                v["near"] = [near, twin_of(near)]
        tick("near")
        part, v["turn"] = mul(v["turn"], *v["near"], integrals, v["near_twin"], [v["b", i] for i in range(last + 1)], 0, 0.5)
        return add(v["turn"], part, [v["sum", i] for i in range(last + 1)])

    return shards


def solution(mesh):
    in_specs = (P("row", ("col", "layer")), P(("row", "layer"), "col"))
    out_specs = P("row", ("col", "layer"))
    R, C, L = (mesh.shape[a] for a in AXES)
    plan = swap_plan(C, L, (128, 128, 128, 128, 128, 128, 128, 128)) if (R, C, L) == (2, 4, 4) else gather_plan
    return jax.shard_map(plan, mesh=mesh, in_specs=in_specs, out_specs=out_specs, check_vma=False)
```

```python
import jax
import jax.numpy as jnp
from jax import lax
from jax.experimental import pallas as pl
from jax.experimental.pallas import tpu as pltpu
from jax.sharding import PartitionSpec as P

AXES = ("row", "col", "layer")
F32, BF16 = jnp.float32, jnp.bfloat16
SMEM = pl.BlockSpec(memory_space=pltpu.SMEM)
ANY = pl.BlockSpec(memory_space=pltpu.HBM)
FREE = pl.CostEstimate(flops=0, bytes_accessed=0, transcendentals=0)
OWN = 0
DEPTH = 3
LAG = 1
MOVED = 3
PAIR = 7
CUTLIM = 62
JOINLIM = 32


def gather_plan(amplitudes, integrals):
    amp_panel = lax.all_gather(amplitudes, "layer", axis=1, tiled=True)
    amp_whole = lax.all_gather(amp_panel, "col", axis=1, tiled=True)
    int_mine = lax.all_to_all(integrals, "layer", split_axis=1, concat_axis=0, tiled=True)
    product = jnp.dot(
        amp_whole,
        lax.all_gather(int_mine, "row", axis=0, tiled=True),
        precision=lax.Precision.HIGHEST,
        preferred_element_type=F32,
    )
    return 0.5 * product


def split(value):
    high = value.astype(BF16)
    return high, (value - high.astype(F32)).astype(BF16)


def copies(pairs, sems):
    made = [pltpu.make_async_copy(src, dst, sems.at[i]) for i, (src, dst) in enumerate(pairs)]
    for copy in made:
        copy.start()
    return made


def cut(integrals, wanted, limit):
    rows, width = integrals.shape[0], integrals.shape[1] // 4
    wide = [sum(n for _, _, n in parts) for parts in wanted]

    def kernel(source, *refs):
        layer = lax.axis_index("layer")
        pairs = []
        for parts, out in zip(wanted, refs):
            to = 0
            for rel, at, n in parts:
                pairs.append((source.at[:, pl.ds(pl.multiple_of((layer ^ rel) * width + at, 128), n)], out.at[:, pl.ds(to, n)]))
                to += n
        for copy in copies(pairs, refs[-1]):
            copy.wait()

    return pl.pallas_call(
        kernel,
        out_shape=[jax.ShapeDtypeStruct((rows, n), F32) for n in wide],
        in_specs=[ANY],
        out_specs=[pl.BlockSpec(memory_space=pltpu.VMEM)] * len(wanted),
        scratch_shapes=[pltpu.SemaphoreType.DMA((sum(len(parts) for parts in wanted),))],
        compiler_params=pltpu.CompilerParams(vmem_limit_bytes=limit << 20),
        cost_estimate=FREE,
        name="cut",
    )(integrals)


def join(integrals, twin, cuts):
    rows, width = integrals.shape[0], integrals.shape[1] // 4

    def kernel(source, theirs, *refs):
        layer = lax.axis_index("layer")
        pairs = []
        for (at, n), out in zip(cuts, refs):
            pairs.append((source.at[:, pl.ds(pl.multiple_of((layer ^ 2) * width + at, 128), n)], out.at[:rows]))
            pairs.append((theirs.at[:, pl.ds(width + at - cuts[0][0], n)], out.at[rows:]))
        for copy in copies(pairs, refs[-1]):
            copy.wait()

    return pl.pallas_call(
        kernel,
        out_shape=[jax.ShapeDtypeStruct((2 * rows, n), F32) for _, n in cuts],
        in_specs=[ANY] * 2,
        out_specs=[pl.BlockSpec(memory_space=pltpu.VMEM)] * len(cuts),
        scratch_shapes=[pltpu.SemaphoreType.DMA((2 * len(cuts),))],
        compiler_params=pltpu.CompilerParams(vmem_limit_bytes=JOINLIM << 20),
        cost_estimate=FREE,
        name="join",
    )(integrals, twin)


def mul(token, blocks, twin, integrals, near, pieces, at, scale):
    _, rows, kb = blocks.shape
    depth, width = integrals.shape[0], integrals.shape[1] // 4
    k = 8 * kb
    n = sum(piece[0].shape[1] for piece in pieces)
    flat = [part for piece in pieces for part in piece]
    count = 8 + 2 * (len(pieces) + 1)

    def kernel(turn, mine, other, source, c1, *refs):
        out, turned, a, b, sems = refs[len(flat) :]
        turned[0] = turn[0]
        layer, p = lax.axis_index("layer"), lax.axis_index("col") % 2
        y, core = layer // 2, layer % 2

        def rows_of(rel):
            return pl.ds(pl.multiple_of((layer ^ rel) * depth, depth), depth)

        pairs = [(source.at[:, pl.ds(pl.multiple_of(layer * width + at, 128), n)], b.at[rows_of(0), :])]
        pairs.append((c1.at[:, pl.ds(at, n)], b.at[rows_of(1), :]))
        to, rest = 0, list(refs)
        for piece in pieces:
            got = [rest.pop(0) for _ in piece]
            wide = piece[0].shape[1]
            c2, c3 = got if len(got) == 2 else (got[0].at[:depth], got[0].at[depth:])
            pairs += [(c2, b.at[rows_of(2), pl.ds(to, wide)]), (c3, b.at[rows_of(3), pl.ds(to, wide)])]
            to += wide
        for rel in range(4):
            slot = (p ^ (rel >> 1)) * 2 + (y ^ (rel & 1))
            for ref, where in ((mine, core), (other, 1 - core)):
                lanes = pl.ds(pl.multiple_of((slot * 2 + where) * kb, kb), kb)
                pairs.append((ref.at[rel], a.at[:, lanes]))
        for copy in copies(pairs, sems):
            copy.wait()
        ah, al = split(a[...])
        for first in range(0, n, 256):
            lanes = pl.ds(first, min(256, n - first))
            bh, bl = split(b[:, lanes])
            out[:, lanes] = scale * (
                jnp.dot(ah, bh, preferred_element_type=F32)
                + jnp.dot(ah, bl, preferred_element_type=F32)
                + jnp.dot(al, bh, preferred_element_type=F32)
            )

    return pl.pallas_call(
        kernel,
        out_shape=(jax.ShapeDtypeStruct((rows, n), F32), jax.ShapeDtypeStruct((1,), jnp.int32)),
        in_specs=[SMEM] + [ANY] * (4 + len(flat)),
        out_specs=(pl.BlockSpec(memory_space=pltpu.VMEM), SMEM),
        scratch_shapes=[pltpu.VMEM((rows, k), F32), pltpu.VMEM((k, n), F32), pltpu.SemaphoreType.DMA((count,))],
        compiler_params=pltpu.CompilerParams(vmem_limit_bytes=24 << 20),
        cost_estimate=pl.CostEstimate(flops=6 * rows * n * k, bytes_accessed=0, transcendentals=0),
        name="mul",
    )(token, blocks, twin, integrals, near, *flat)


def add(token, mine, others):
    rows, width = mine.shape
    starts = [sum(o.shape[1] for o in others[:i]) for i in range(len(others))]

    def kernel(turn, a, *refs):
        sources, out, total, sems = refs[: len(others)], refs[-3], refs[-2], refs[-1]
        made = []
        for i, (source, at) in enumerate(zip(sources, starts)):
            lanes = pl.ds(at, others[i].shape[1])
            total[:, lanes] = a[:, lanes] + 0.5 * source[...]
            made.append(pltpu.make_async_copy(total.at[:, lanes], out.at[:, lanes], sems.at[i]))
            made[-1].start()
        for copy in made:
            copy.wait()

    return pl.pallas_call(
        kernel,
        out_shape=jax.ShapeDtypeStruct((rows, width), F32),
        in_specs=[SMEM] + [pl.BlockSpec(memory_space=pltpu.VMEM)] * (1 + len(others)),
        out_specs=ANY,
        scratch_shapes=[pltpu.VMEM((rows, width), F32), pltpu.SemaphoreType.DMA((len(others),))],
        compiler_params=pltpu.CompilerParams(vmem_limit_bytes=24 << 20),
        cost_estimate=FREE,
        name="add",
    )(token, mine, *others)


def swap_plan(C, L, cuts):
    half = C // 2
    every = [(r, c, l) for r in range(2) for c in range(C) for l in range(L)]

    def flat(r, c, l):
        return (r * C + c) * L + l

    def send(value, where, who=lambda r, c, l: True):
        return lax.ppermute(value, AXES, [(flat(*d), flat(*where(*d))) for d in every if who(*d)])

    def home(r, c, l):
        return c // half == r

    def away(r, c, l):
        return c // half != r

    def shards(amplitudes, integrals):
        r, c, l = (lax.axis_index(a) for a in AXES)
        here = c // half == r
        width = integrals.shape[1] // L
        starts = [sum(cuts[:i]) for i in range(len(cuts))]
        last = len(cuts) - 1
        v = {"turn": r.reshape(1).astype(jnp.int32)}

        def tick(*names):
            names = ("turn", *names)
            v.update(zip(names, lax.optimization_barrier([v[name] for name in names])))

        def now(*names):
            tick(*names)
            return v[names[0]] if len(names) == 1 else [v[name] for name in names]

        def twin_of(value):
            return send(value, lambda r, c, l: (r, c, l ^ 1))

        def far_sum(i):
            part, v["turn"] = mul(v["turn"], *v["far"], integrals, v["near_twin"], [v["b", i]], starts[i], 1.0)
            v["sum", i] = send(part, lambda r, c, l: (1 - r, c, l))

        def go(i):
            v["b", i] = [send(now(("slab", i)), lambda r, c, l: (r, c, l ^ 2))]

        v["straight"] = send(amplitudes, lambda r, c, l: (1 - r, c, l), away)
        v["slant"] = send(amplitudes, lambda r, c, l: (1 - r, (c + half) % C, l), away)
        *first, rest = cut(integrals, [[(rel, 0, cuts[0])] for rel in (2, 3)] + [[(1, 0, width), (3, cuts[0], width - cuts[0])]], CUTLIM)
        v["b", 0] = [send(part, lambda r, c, l, rel=rel: (r, c, l ^ rel)) for rel, part in zip((2, 3), first)]
        v["rest"], v["amp"] = lax.optimization_barrier((rest, amplitudes))
        v["turned"] = send(amplitudes, lambda r, c, l: (r, c, l ^ 2), home)
        tick("straight", "slant", ("b", 0), "turned", "rest", "amp")
        other = jnp.where(here, v["straight"], v["slant"])
        v["blocks"] = [other] + [
            send(other, lambda r, c, l, p=p, y=y: (r, c ^ p, l ^ (2 * y))) for p, y in ((0, 1), (1, 0), (1, 1))
        ]
        v["near_twin"] = twin_of(v["rest"])
        slabs = join(integrals, v["near_twin"], [(starts[i], cuts[i]) for i in range(1, last + 1)])
        v.update({("slab", i + 1): slab for i, slab in enumerate(slabs)})
        tick("blocks", "near_twin", "turned", "amp", *[("slab", i) for i in range(1, last + 1)])
        far = jnp.stack(v["blocks"])
        v["far"] = [far, twin_of(far)]
        for i in range(1, DEPTH):
            go(i)
        tick("far")
        for i in range(last + 1):
            if i:
                tick(("b", i))
            if i + DEPTH <= last:
                go(i + DEPTH)
            far_sum(i)
            if i == OWN:
                v["own"] = jnp.stack(now("amp", "turned"))
                v["moved"] = send(v["own"], lambda r, c, l: (r, (c + half) % C, l), home)
            if i >= LAG:
                tick(("sum", i - LAG))
            if i == MOVED:
                tick("moved")
                v["own"] = jnp.where(here, *now("own", "moved"))
                v["pair"] = send(v["own"], lambda r, c, l: (r, c ^ 1, l))
            if i == PAIR:
                tick("pair")
                near = jnp.concatenate(now("own", "pair"))
                v["near"] = [near, twin_of(near)]
        tick("near")
        part, v["turn"] = mul(v["turn"], *v["near"], integrals, v["near_twin"], [v["b", i] for i in range(last + 1)], 0, 0.5)
        return add(v["turn"], part, [v["sum", i] for i in range(last + 1)])

    return shards


def solution(mesh):
    in_specs = (P("row", ("col", "layer")), P(("row", "layer"), "col"))
    out_specs = P("row", ("col", "layer"))
    R, C, L = (mesh.shape[a] for a in AXES)
    plan = swap_plan(C, L, (128, 128, 128, 128, 128, 128, 128, 128)) if (R, C, L) == (2, 4, 4) else gather_plan
    return jax.shard_map(plan, mesh=mesh, in_specs=in_specs, out_specs=out_specs, check_vma=False)
```

```python
import jax
import jax.numpy as jnp
from jax import lax
from jax.experimental import pallas as pl
from jax.experimental.pallas import tpu as pltpu
from jax.sharding import PartitionSpec as P

AXES = ("row", "col", "layer")
F32, BF16 = jnp.float32, jnp.bfloat16
SMEM = pl.BlockSpec(memory_space=pltpu.SMEM)
ANY = pl.BlockSpec(memory_space=pltpu.HBM)
FREE = pl.CostEstimate(flops=0, bytes_accessed=0, transcendentals=0)
OWN = 0
DEPTH = 4
LAG = 1
MOVED = 3
PAIR = 5
CUTLIM = 62
JOINLIM = 32
SOME = pl.CostEstimate(flops=4 * 10**8, bytes_accessed=0, transcendentals=0)


def gather_plan(amplitudes, integrals):
    amp_panel = lax.all_gather(amplitudes, "layer", axis=1, tiled=True)
    amp_whole = lax.all_gather(amp_panel, "col", axis=1, tiled=True)
    int_mine = lax.all_to_all(integrals, "layer", split_axis=1, concat_axis=0, tiled=True)
    product = jnp.dot(
        amp_whole,
        lax.all_gather(int_mine, "row", axis=0, tiled=True),
        precision=lax.Precision.HIGHEST,
        preferred_element_type=F32,
    )
    return 0.5 * product


def split(value):
    high = value.astype(BF16)
    return high, (value - high.astype(F32)).astype(BF16)


def copies(pairs, sems):
    made = [pltpu.make_async_copy(src, dst, sems.at[i]) for i, (src, dst) in enumerate(pairs)]
    for copy in made:
        copy.start()
    return made


def cut(integrals, wanted, limit):
    rows, width = integrals.shape[0], integrals.shape[1] // 4
    wide = [sum(n for _, _, n in parts) for parts in wanted]

    def kernel(source, *refs):
        layer = lax.axis_index("layer")
        pairs = []
        for parts, out in zip(wanted, refs):
            to = 0
            for rel, at, n in parts:
                pairs.append((source.at[:, pl.ds(pl.multiple_of((layer ^ rel) * width + at, 128), n)], out.at[:, pl.ds(to, n)]))
                to += n
        for copy in copies(pairs, refs[-1]):
            copy.wait()

    return pl.pallas_call(
        kernel,
        out_shape=[jax.ShapeDtypeStruct((rows, n), F32) for n in wide],
        in_specs=[ANY],
        out_specs=[pl.BlockSpec(memory_space=pltpu.VMEM)] * len(wanted),
        scratch_shapes=[pltpu.SemaphoreType.DMA((sum(len(parts) for parts in wanted),))],
        compiler_params=pltpu.CompilerParams(vmem_limit_bytes=limit << 20),
        cost_estimate=FREE,
        name="cut",
    )(integrals)


def join(integrals, twin, cuts):
    rows, width = integrals.shape[0], integrals.shape[1] // 4

    def kernel(source, theirs, *refs):
        layer = lax.axis_index("layer")
        pairs = []
        for (at, n), out in zip(cuts, refs):
            pairs.append((source.at[:, pl.ds(pl.multiple_of((layer ^ 2) * width + at, 128), n)], out.at[:rows]))
            pairs.append((theirs.at[:, pl.ds(width + at - cuts[0][0], n)], out.at[rows:]))
        for copy in copies(pairs, refs[-1]):
            copy.wait()

    return pl.pallas_call(
        kernel,
        out_shape=[jax.ShapeDtypeStruct((2 * rows, n), F32) for _, n in cuts],
        in_specs=[ANY] * 2,
        out_specs=[pl.BlockSpec(memory_space=pltpu.VMEM)] * len(cuts),
        scratch_shapes=[pltpu.SemaphoreType.DMA((2 * len(cuts),))],
        compiler_params=pltpu.CompilerParams(vmem_limit_bytes=JOINLIM << 20),
        cost_estimate=FREE,
        name="join",
    )(integrals, twin)


def mul(token, blocks, twin, integrals, near, pieces, at, scale, cost=None, sums=()):
    _, rows, kb = blocks.shape
    depth, width = integrals.shape[0], integrals.shape[1] // 4
    k = 8 * kb
    n = sum(piece[0].shape[1] for piece in pieces)
    flat = [part for piece in pieces for part in piece]
    done = sum(part.shape[1] for part in sums)
    count = 8 + 2 * (len(pieces) + 1) + len(sums)

    def kernel(turn, mine, other, source, c1, *refs):
        out, turned, a, b, sems, *more = refs[len(flat) + len(sums) :]
        others = refs[len(flat) : len(flat) + len(sums)]
        turned[0] = turn[0]
        layer, p = lax.axis_index("layer"), lax.axis_index("col") % 2
        y, core = layer // 2, layer % 2

        def rows_of(rel):
            return pl.ds(pl.multiple_of((layer ^ rel) * depth, depth), depth)

        pairs = [(source.at[:, pl.ds(pl.multiple_of(layer * width + at, 128), n)], b.at[rows_of(0), :])]
        pairs.append((c1.at[:, pl.ds(at, n)], b.at[rows_of(1), :]))
        to, rest = 0, list(refs)
        for piece in pieces:
            got = [rest.pop(0) for _ in piece]
            wide = piece[0].shape[1]
            c2, c3 = got if len(got) == 2 else (got[0].at[:depth], got[0].at[depth:])
            pairs += [(c2, b.at[rows_of(2), pl.ds(to, wide)]), (c3, b.at[rows_of(3), pl.ds(to, wide)])]
            to += wide
        for rel in range(4):
            slot = (p ^ (rel >> 1)) * 2 + (y ^ (rel & 1))
            for ref, where in ((mine, core), (other, 1 - core)):
                lanes = pl.ds(pl.multiple_of((slot * 2 + where) * kb, kb), kb)
                pairs.append((ref.at[rel], a.at[:, lanes]))
        to = 0
        for other_sum, part in zip(others, sums):
            pairs.append((other_sum, more[0].at[:, pl.ds(to, part.shape[1])]))
            to += part.shape[1]
        for copy in copies(pairs, sems):
            copy.wait()
        ah, al = split(a[...])
        for first in range(0, n, 256):
            lanes = pl.ds(first, min(256, n - first))
            bh, bl = split(b[:, lanes])
            total = (
                jnp.dot(ah, bh, preferred_element_type=F32)
                + jnp.dot(ah, bl, preferred_element_type=F32)
                + jnp.dot(al, bh, preferred_element_type=F32)
            )
            if first < done:
                total += more[0][:, lanes]
            out[:, lanes] = scale * total

    return pl.pallas_call(
        kernel,
        out_shape=(jax.ShapeDtypeStruct((rows, n), F32), jax.ShapeDtypeStruct((1,), jnp.int32)),
        in_specs=[SMEM] + [ANY] * (4 + len(flat) + len(sums)),
        out_specs=(pl.BlockSpec(memory_space=pltpu.VMEM), SMEM),
        scratch_shapes=[pltpu.VMEM((rows, k), F32), pltpu.VMEM((k, n), F32), pltpu.SemaphoreType.DMA((count,))]
        + [pltpu.VMEM((rows, done), F32)] * bool(done),
        compiler_params=pltpu.CompilerParams(vmem_limit_bytes=24 << 20),
        cost_estimate=SOME if cost is None else cost,
        name="mul",
    )(token, blocks, twin, integrals, near, *flat, *sums)


def swap_plan(C, L, eighths):
    half = C // 2
    every = [(r, c, l) for r in range(2) for c in range(C) for l in range(L)]

    def flat(r, c, l):
        return (r * C + c) * L + l

    def send(value, where, who=lambda r, c, l: True):
        return lax.ppermute(value, AXES, [(flat(*d), flat(*where(*d))) for d in every if who(*d)])

    def home(r, c, l):
        return c // half == r

    def away(r, c, l):
        return c // half != r

    def shards(amplitudes, integrals):
        r, c, l = (lax.axis_index(a) for a in AXES)
        here = c // half == r
        width = integrals.shape[1] // L
        cuts = [width * part // 8 for part in eighths]
        starts = [sum(cuts[:i]) for i in range(len(cuts))]
        last = len(cuts) - 1
        v = {"turn": r.reshape(1).astype(jnp.int32)}

        def tick(*names):
            names = ("turn", *names)
            v.update(zip(names, lax.optimization_barrier([v[name] for name in names])))

        def now(*names):
            tick(*names)
            return v[names[0]] if len(names) == 1 else [v[name] for name in names]

        def twin_of(value):
            return send(value, lambda r, c, l: (r, c, l ^ 1))

        def far_sum(i):
            part, v["turn"] = mul(v["turn"], *v["far"], integrals, v["near_twin"], [v["b", i]], starts[i], 1.0)
            v["sum", i] = send(part, lambda r, c, l: (1 - r, c, l))

        def go(i):
            v["b", i] = [send(now(("slab", i)), lambda r, c, l: (r, c, l ^ 2))]

        v["straight"] = send(amplitudes, lambda r, c, l: (1 - r, c, l), away)
        v["slant"] = send(amplitudes, lambda r, c, l: (1 - r, (c + half) % C, l), away)
        *first, rest = cut(integrals, [[(rel, 0, cuts[0])] for rel in (2, 3)] + [[(1, 0, width), (3, cuts[0], width - cuts[0])]], CUTLIM)
        v["b", 0] = [send(part, lambda r, c, l, rel=rel: (r, c, l ^ rel)) for rel, part in zip((2, 3), first)]
        v["rest"], v["amp"] = lax.optimization_barrier((rest, amplitudes))
        v["turned"] = send(amplitudes, lambda r, c, l: (r, c, l ^ 2), home)
        tick("straight", "slant", ("b", 0), "turned", "rest", "amp")
        other = jnp.where(here, v["straight"], v["slant"])
        v["blocks"] = [other] + [
            send(other, lambda r, c, l, p=p, y=y: (r, c ^ p, l ^ (2 * y))) for p, y in ((0, 1), (1, 0), (1, 1))
        ]
        v["near_twin"] = twin_of(v["rest"])
        slabs = join(integrals, v["near_twin"], [(starts[i], cuts[i]) for i in range(1, last + 1)])
        v.update({("slab", i + 1): slab for i, slab in enumerate(slabs)})
        tick("blocks", "near_twin", "turned", "amp", *[("slab", i) for i in range(1, last + 1)])
        far = jnp.stack(v["blocks"])
        v["far"] = [far, twin_of(far)]
        for i in range(1, DEPTH):
            go(i)
        tick("far")
        for i in range(last + 1):
            if i:
                tick(("b", i))
            if i + DEPTH <= last:
                go(i + DEPTH)
            far_sum(i)
            if i == OWN:
                v["own"] = jnp.stack(now("amp", "turned"))
                v["moved"] = send(v["own"], lambda r, c, l: (r, (c + half) % C, l), home)
            if i >= LAG:
                tick(("sum", i - LAG))
            if i == MOVED:
                tick("moved")
                v["own"] = jnp.where(here, *now("own", "moved"))
                v["pair"] = send(v["own"], lambda r, c, l: (r, c ^ 1, l))
            if i == PAIR:
                tick("pair")
                near = jnp.concatenate(now("own", "pair"))
                v["near"] = [near, twin_of(near)]
        tick("near")
        part, v["turn"] = mul(v["turn"], *v["near"], integrals, v["near_twin"], [v["b", i] for i in range(last + 1)], 0, 0.5, FREE, [v["sum", i] for i in range(last)])
        return lax.dynamic_update_slice(part, part[:, starts[last] :] + 0.5 * v["sum", last], (0, starts[last]))

    return shards


def solution(mesh):
    in_specs = (P("row", ("col", "layer")), P(("row", "layer"), "col"))
    out_specs = P("row", ("col", "layer"))
    R, C, L = (mesh.shape[a] for a in AXES)
    plan = swap_plan(C, L, (1, 1, 1, 2, 1, 2)) if (R, C, L) == (2, 4, 4) else gather_plan
    return jax.shard_map(plan, mesh=mesh, in_specs=in_specs, out_specs=out_specs, check_vma=False)
```

```python
import jax
import jax.numpy as jnp
from jax import lax
from jax.experimental import pallas as pl
from jax.experimental.pallas import tpu as pltpu
from jax.sharding import PartitionSpec as P

AXES = ("row", "col", "layer")
F32, BF16 = jnp.float32, jnp.bfloat16
SMEM = pl.BlockSpec(memory_space=pltpu.SMEM)
ANY = pl.BlockSpec(memory_space=pltpu.HBM)
FREE = pl.CostEstimate(flops=0, bytes_accessed=0, transcendentals=0)
OWN = 0
DEPTH = 4
LAG = 1
MOVED = 3
PAIR = 5
CUTLIM = 62
JOINLIM = 32
SOME = pl.CostEstimate(flops=4 * 10**8, bytes_accessed=0, transcendentals=0)


def gather_plan(amplitudes, integrals):
    amp_panel = lax.all_gather(amplitudes, "layer", axis=1, tiled=True)
    amp_whole = lax.all_gather(amp_panel, "col", axis=1, tiled=True)
    int_mine = lax.all_to_all(integrals, "layer", split_axis=1, concat_axis=0, tiled=True)
    product = jnp.dot(
        amp_whole,
        lax.all_gather(int_mine, "row", axis=0, tiled=True),
        precision=lax.Precision.HIGHEST,
        preferred_element_type=F32,
    )
    return 0.5 * product


def split(value):
    high = value.astype(BF16)
    return high, (value - high.astype(F32)).astype(BF16)


def copies(pairs, sems):
    made = [pltpu.make_async_copy(src, dst, sems.at[i]) for i, (src, dst) in enumerate(pairs)]
    for copy in made:
        copy.start()
    return made


def cut(integrals, wanted, limit):
    rows, width = integrals.shape[0], integrals.shape[1] // 4
    wide = [sum(n for _, _, n in parts) for parts in wanted]

    def kernel(source, *refs):
        layer = lax.axis_index("layer")
        pairs = []
        for parts, out in zip(wanted, refs):
            to = 0
            for rel, at, n in parts:
                pairs.append((source.at[:, pl.ds(pl.multiple_of((layer ^ rel) * width + at, 128), n)], out.at[:, pl.ds(to, n)]))
                to += n
        for copy in copies(pairs, refs[-1]):
            copy.wait()

    return pl.pallas_call(
        kernel,
        out_shape=[jax.ShapeDtypeStruct((rows, n), F32) for n in wide],
        in_specs=[ANY],
        out_specs=[pl.BlockSpec(memory_space=pltpu.VMEM)] * len(wanted),
        scratch_shapes=[pltpu.SemaphoreType.DMA((sum(len(parts) for parts in wanted),))],
        compiler_params=pltpu.CompilerParams(vmem_limit_bytes=limit << 20),
        cost_estimate=FREE,
        name="cut",
    )(integrals)


def join(integrals, twin, cuts):
    rows, width = integrals.shape[0], integrals.shape[1] // 4

    def kernel(source, theirs, *refs):
        layer = lax.axis_index("layer")
        pairs = []
        for (at, n), out in zip(cuts, refs):
            pairs.append((source.at[:, pl.ds(pl.multiple_of((layer ^ 2) * width + at, 128), n)], out.at[:rows]))
            pairs.append((theirs.at[:, pl.ds(width + at - cuts[0][0], n)], out.at[rows:]))
        for copy in copies(pairs, refs[-1]):
            copy.wait()

    return pl.pallas_call(
        kernel,
        out_shape=[jax.ShapeDtypeStruct((2 * rows, n), F32) for _, n in cuts],
        in_specs=[ANY] * 2,
        out_specs=[pl.BlockSpec(memory_space=pltpu.VMEM)] * len(cuts),
        scratch_shapes=[pltpu.SemaphoreType.DMA((2 * len(cuts),))],
        compiler_params=pltpu.CompilerParams(vmem_limit_bytes=JOINLIM << 20),
        cost_estimate=FREE,
        name="join",
    )(integrals, twin)


def mul(token, blocks, twin, integrals, near, pieces, at, scale, cost=None, sums=()):
    _, rows, kb = blocks.shape
    depth, width = integrals.shape[0], integrals.shape[1] // 4
    k = 8 * kb
    n = sum(piece[0].shape[1] for piece in pieces)
    flat = [part for piece in pieces for part in piece]
    done = sum(part.shape[1] for part in sums)
    count = 8 + 2 * (len(pieces) + 1) + len(sums)

    def kernel(turn, mine, other, source, c1, *refs):
        out, turned, a, b, sems, *more = refs[len(flat) + len(sums) :]
        others = refs[len(flat) : len(flat) + len(sums)]
        turned[0] = turn[0]
        layer, p = lax.axis_index("layer"), lax.axis_index("col") % 2
        y, core = layer // 2, layer % 2

        def rows_of(rel):
            return pl.ds(pl.multiple_of((layer ^ rel) * depth, depth), depth)

        pairs = [(source.at[:, pl.ds(pl.multiple_of(layer * width + at, 128), n)], b.at[rows_of(0), :])]
        pairs.append((c1.at[:, pl.ds(at, n)], b.at[rows_of(1), :]))
        to, rest = 0, list(refs)
        for piece in pieces:
            got = [rest.pop(0) for _ in piece]
            wide = piece[0].shape[1]
            c2, c3 = got if len(got) == 2 else (got[0].at[:depth], got[0].at[depth:])
            pairs += [(c2, b.at[rows_of(2), pl.ds(to, wide)]), (c3, b.at[rows_of(3), pl.ds(to, wide)])]
            to += wide
        for rel in range(4):
            slot = (p ^ (rel >> 1)) * 2 + (y ^ (rel & 1))
            for ref, where in ((mine, core), (other, 1 - core)):
                lanes = pl.ds(pl.multiple_of((slot * 2 + where) * kb, kb), kb)
                pairs.append((ref.at[rel], a.at[:, lanes]))
        to = 0
        for other_sum, part in zip(others, sums):
            pairs.append((other_sum, more[0].at[:, pl.ds(to, part.shape[1])]))
            to += part.shape[1]
        made = copies(pairs, sems)
        early = 2 + 2 * len(pieces)
        for copy in made[:early]:
            copy.wait()
        if len(pieces) == 1:
            bh, bl = split(b[...])
        for copy in made[early:]:
            copy.wait()
        ah, al = split(a[...])
        for first in range(0, n, 256):
            lanes = pl.ds(first, min(256, n - first))
            if len(pieces) > 1:
                bh, bl = split(b[:, lanes])
            total = (
                jnp.dot(ah, bh, preferred_element_type=F32)
                + jnp.dot(ah, bl, preferred_element_type=F32)
                + jnp.dot(al, bh, preferred_element_type=F32)
            )
            if first < done:
                total += more[0][:, lanes]
            out[:, lanes] = scale * total

    return pl.pallas_call(
        kernel,
        out_shape=(jax.ShapeDtypeStruct((rows, n), F32), jax.ShapeDtypeStruct((1,), jnp.int32)),
        in_specs=[SMEM] + [ANY] * (4 + len(flat) + len(sums)),
        out_specs=(pl.BlockSpec(memory_space=pltpu.VMEM), SMEM),
        scratch_shapes=[pltpu.VMEM((rows, k), F32), pltpu.VMEM((k, n), F32), pltpu.SemaphoreType.DMA((count,))]
        + [pltpu.VMEM((rows, done), F32)] * bool(done),
        compiler_params=pltpu.CompilerParams(vmem_limit_bytes=24 << 20),
        cost_estimate=SOME if cost is None else cost,
        name="mul",
    )(token, blocks, twin, integrals, near, *flat, *sums)


def swap_plan(C, L, eighths):
    half = C // 2
    every = [(r, c, l) for r in range(2) for c in range(C) for l in range(L)]

    def flat(r, c, l):
        return (r * C + c) * L + l

    def send(value, where, who=lambda r, c, l: True):
        return lax.ppermute(value, AXES, [(flat(*d), flat(*where(*d))) for d in every if who(*d)])

    def home(r, c, l):
        return c // half == r

    def away(r, c, l):
        return c // half != r

    def shards(amplitudes, integrals):
        r, c, l = (lax.axis_index(a) for a in AXES)
        here = c // half == r
        width = integrals.shape[1] // L
        cuts = [width * part // 8 for part in eighths]
        starts = [sum(cuts[:i]) for i in range(len(cuts))]
        last = len(cuts) - 1
        v = {"turn": r.reshape(1).astype(jnp.int32)}

        def tick(*names):
            names = ("turn", *names)
            v.update(zip(names, lax.optimization_barrier([v[name] for name in names])))

        def now(*names):
            tick(*names)
            return v[names[0]] if len(names) == 1 else [v[name] for name in names]

        def twin_of(value):
            return send(value, lambda r, c, l: (r, c, l ^ 1))

        def far_sum(i):
            part, v["turn"] = mul(v["turn"], *v["far"], integrals, v["near_twin"], [v["b", i]], starts[i], 1.0)
            v["sum", i] = send(part, lambda r, c, l: (1 - r, c, l))

        def go(i):
            v["b", i] = [send(now(("slab", i)), lambda r, c, l: (r, c, l ^ 2))]

        v["straight"] = send(amplitudes, lambda r, c, l: (1 - r, c, l), away)
        v["slant"] = send(amplitudes, lambda r, c, l: (1 - r, (c + half) % C, l), away)
        *first, rest = cut(integrals, [[(rel, 0, cuts[0])] for rel in (2, 3)] + [[(1, 0, width), (3, cuts[0], width - cuts[0])]], CUTLIM)
        v["b", 0] = [send(part, lambda r, c, l, rel=rel: (r, c, l ^ rel)) for rel, part in zip((2, 3), first)]
        v["rest"], v["amp"] = lax.optimization_barrier((rest, amplitudes))
        v["turned"] = send(amplitudes, lambda r, c, l: (r, c, l ^ 2), home)
        tick("straight", "slant", ("b", 0), "turned", "rest", "amp")
        other = jnp.where(here, v["straight"], v["slant"])
        v["blocks"] = [other] + [
            send(other, lambda r, c, l, p=p, y=y: (r, c ^ p, l ^ (2 * y))) for p, y in ((0, 1), (1, 0), (1, 1))
        ]
        v["near_twin"] = twin_of(v["rest"])
        slabs = join(integrals, v["near_twin"], [(starts[i], cuts[i]) for i in range(1, last + 1)])
        v.update({("slab", i + 1): slab for i, slab in enumerate(slabs)})
        tick("blocks", "near_twin", "turned", "amp", *[("slab", i) for i in range(1, last + 1)])
        far = jnp.stack(v["blocks"])
        v["far"] = [far, twin_of(far)]
        for i in range(1, DEPTH):
            go(i)
        tick("far")
        for i in range(last + 1):
            if i:
                tick(("b", i))
            if i + DEPTH <= last:
                go(i + DEPTH)
            far_sum(i)
            if i == OWN:
                v["own"] = jnp.stack(now("amp", "turned"))
                v["moved"] = send(v["own"], lambda r, c, l: (r, (c + half) % C, l), home)
            if i >= LAG:
                tick(("sum", i - LAG))
            if i == MOVED:
                tick("moved")
                v["own"] = jnp.where(here, *now("own", "moved"))
                v["pair"] = send(v["own"], lambda r, c, l: (r, c ^ 1, l))
            if i == PAIR:
                tick("pair")
                near = jnp.concatenate(now("own", "pair"))
                v["near"] = [near, twin_of(near)]
        tick("near")
        part, v["turn"] = mul(v["turn"], *v["near"], integrals, v["near_twin"], [v["b", i] for i in range(last + 1)], 0, 0.5, FREE, [v["sum", i] for i in range(last)])
        return lax.dynamic_update_slice(part, part[:, starts[last] :] + 0.5 * v["sum", last], (0, starts[last]))

    return shards


def solution(mesh):
    in_specs = (P("row", ("col", "layer")), P(("row", "layer"), "col"))
    out_specs = P("row", ("col", "layer"))
    R, C, L = (mesh.shape[a] for a in AXES)
    plan = swap_plan(C, L, (1, 1, 1, 2, 1, 2)) if (R, C, L) == (2, 4, 4) else gather_plan
    return jax.shard_map(plan, mesh=mesh, in_specs=in_specs, out_specs=out_specs, check_vma=False)
```
